256 devices in a mesh: row: 16 (over y, z_lo, core), col: 16 (over x, z_hi).
Axes of the slice: x: 4, y: 4, z: 8 (z_hi: 4, z_lo: 2; z = z_hi * 2 + z_lo), core: 2. Of those that a mesh axis runs over, the one named last changes fastest.
Arguments:
- features: float32 [65536, 256], P(('col', 'row')), may hold values from -6 to 6
- w_self: float32 [256, 256], replicated, may hold values from -0.375 to 0.375
- w_neigh: float32 [256, 256], replicated, may hold values from -0.375 to 0.375
- upstream: float32 [65536, 256], P(('row', 'col')), may hold values from -6 to 6
- tile_coords: int32 [16, 16, 192, 2], P('row', 'col'), may hold values from 0 to 31, as said below
- tile_count: int32 [16, 16], P('row', 'col'), may hold values from 1 to 192, as said below
- tile_bits: int32 [16, 16, 192, 16, 128], P('row', 'col'), may hold values from 0 to 255
Outputs:
- hidden: float32 [65536, 256], P(('row', 'col'))
- grad_features: float32 [65536, 256], P(('col', 'row'))
- grad_self: float32 [256, 256], replicated
- grad_neigh: float32 [256, 256], replicated
The draws below stay inside these ranges and needn't reach their ends.
Inputs may be any that keep to these rules, and one draw needn't show every extreme that they name: tile_coords[r, c, t, 0] is a block of 128 nodes within the 4096 nodes of row part r, tile_coords[r, c, t, 1] one within the 4096 nodes of column part c; the slots of one device name distinct block pairs; slots at or past tile_count[r, c] carry coordinates and bits that are not part of the adjacency. `tile_count`: some device is full in every draw.
All inputs are finite; a program needn't handle non-finite values.
Results may differ from the reference program's by a relative error of at most 0.0003.
Values sent between devices are 32-bit elements; how exact they have to be, the bound alone decides.
No kernel may reach another device: no remote copies, remote signals or barrier semaphores. Data moves between devices by JAX's collectives and lax.ppermute only.
A program may use at most 128 MiB of HBM per device.

```python
import jax
import jax.numpy as jnp
from jax import lax

F = 256
ROWS_DEV = 256
NODES = 65536
TILES = 192
N_ROW = 16
N_COL = 16


def block_layout(key):
    row_blocks = ROWS_DEV * N_COL // 128
    column_blocks = ROWS_DEV * N_ROW // 128
    device_keys = jax.random.split(key, N_ROW * N_COL)

    def per_device(device_key):
        order = jax.random.permutation(device_key, row_blocks * column_blocks)[:TILES]
        return jnp.stack([order // column_blocks, order % column_blocks], axis=-1).astype(jnp.int32)
    return jax.vmap(per_device)(device_keys).reshape(N_ROW, N_COL, TILES, 2)


def draw_tile_coords(key, part):
    layout = block_layout(key)
    return layout


def draw_tile_count(key, part):
    key = jax.random.fold_in(key, 3)
    counts = jax.random.randint(key, (N_ROW * N_COL,), 1, TILES + 1)
    busiest = jax.random.randint(jax.random.fold_in(key, 4), (), 0, N_ROW * N_COL)
    counts = counts.at[busiest].set(TILES)
    return counts.reshape(N_ROW, N_COL).astype(jnp.int32)


def draw_tile_bits(key, part):
    layout = block_layout(key)
    key = jax.random.fold_in(key, 2)
    column_blocks = ROWS_DEV * N_ROW // 128
    total_columns = column_blocks * N_COL
    row_part = ROWS_DEV * N_COL
    weights = jnp.left_shift(jnp.ones((8,), jnp.int32), jnp.arange(8, dtype=jnp.int32))

    def per_device(device_index):
        row_index = device_index // N_COL
        col_index = device_index % N_COL
        coordinates = layout[row_index, col_index]
        column_block = col_index * column_blocks + coordinates[:, 1]
        threshold = 15729 * (total_columns + 2 * column_block) // (2 * total_columns)
        node_row = row_index * row_part + coordinates[:, 0:1] * 128 + jnp.arange(128, dtype=jnp.int32)[None, :]
        isolated = node_row % 97 == 0
        threshold = jnp.where(isolated[:, :, None], 0, threshold[:, None, None])
        random_ints = jax.random.randint(jax.random.fold_in(key, device_index), (TILES, 128, 128), 0, 1048576)
        edge_bits = (random_ints < threshold).astype(jnp.int32)
        packed = jnp.sum(edge_bits.reshape(TILES, 128, 16, 8) * weights, axis=-1, dtype=jnp.int32)
        return jnp.swapaxes(packed, -1, -2)
    stacked = lax.map(per_device, jnp.arange(N_ROW * N_COL, dtype=jnp.int32))
    return stacked.reshape(N_ROW, N_COL, TILES, 16, 128)


def block_scale(own_key, shape, cuts, low, top_value):
    loudness, own = 1.0, jax.random.fold_in(own_key, 6)
    for position, parts in cuts:
        draws = jnp.exp(jax.random.uniform(jax.random.fold_in(own, position), (parts,), jnp.float32, low / len(cuts), top_value / len(cuts)))
        loudness = loudness * jnp.repeat(draws, shape[position] // parts).reshape([-1 if axis == position else 1 for axis in range(len(shape))])
    return loudness


def noise(own_key, dims, width, most, shards=(), kind=jnp.bfloat16):
    gain = block_scale(own_key, dims, shards, -0.22, 0.18) if shards else 1.0
    values = jax.random.normal(own_key, dims, jnp.float32) * width * gain
    return jnp.minimum(jnp.maximum(values, -most), most).astype(kind)


def setup_inputs(seed: int = 0) -> dict:
    key_list = jax.random.split(jax.random.key(seed), 8)
    return {
        "features": noise(key_list[0], (NODES, F), 1.0, 6.0, ((0, 256),), jnp.float32),
        "w_self": noise(key_list[1], (F, F), F ** -0.5, 0.375, (), jnp.float32),
        "w_neigh": noise(key_list[2], (F, F), F ** -0.5, 0.375, (), jnp.float32),
        "upstream": noise(key_list[3], (NODES, F), 1.0, 6.0, ((0, 256),), jnp.float32),
        "tile_coords": draw_tile_coords(jax.random.fold_in(key_list[7], 71), 0),
        "tile_count": draw_tile_count(jax.random.fold_in(key_list[7], 71), 0),
        "tile_bits": draw_tile_bits(jax.random.fold_in(key_list[7], 71), 0),
    }


HIGHEST = lax.Precision.HIGHEST


def unpack_tiles(packed):
    shifts = jnp.arange(8, dtype=jnp.int32)
    spread = (packed[..., :, None, :] >> shifts[None, :, None]) & 1
    spread = spread.reshape(packed.shape[:-2] + (128, 128))
    return jnp.swapaxes(spread, -1, -2).astype(jnp.float32)


def propagate(tile_coords, tile_count, tile_bits, source, transposed):
    block_total = NODES // 128
    row_blocks = NODES // N_ROW // 128
    column_blocks = NODES // N_COL // 128
    shaped = source.reshape(block_total, 128, F)

    def advance(state_pair, device_index):
        running, degree = state_pair
        row_index = device_index // N_COL
        col_index = device_index % N_COL
        coordinates = tile_coords[row_index, col_index]
        live_mask = (jnp.arange(TILES, dtype=jnp.int32) < tile_count[row_index, col_index]).astype(jnp.float32)
        squares = unpack_tiles(tile_bits[row_index, col_index]) * live_mask[:, None, None]
        row_block = (row_index * row_blocks + coordinates[:, 0]).astype(jnp.int32)
        column_block = (col_index * column_blocks + coordinates[:, 1]).astype(jnp.int32)
        if transposed:
            picked = shaped[row_block]
            product = jnp.einsum("tij,tif->tjf", squares, picked, precision=HIGHEST)
            running = running.at[column_block].add(product)
        else:
            picked = shaped[column_block]
            product = jnp.einsum("tij,tjf->tif", squares, picked, precision=HIGHEST)
            running = running.at[row_block].add(product)
            degree = degree.at[row_block].add(jnp.sum(squares, axis=2))
        return (running, degree), None

    start = (jnp.zeros((block_total, 128, F), jnp.float32), jnp.zeros((block_total, 128), jnp.float32))
    (running, degree), _ = lax.scan(advance, start, jnp.arange(N_ROW * N_COL, dtype=jnp.int32))
    return running.reshape(NODES, F), degree.reshape(NODES)


def reference(features, w_self, w_neigh, upstream, tile_coords, tile_count, tile_bits):
    summed, degree = propagate(tile_coords, tile_count, tile_bits, features, False)
    inverse = 1.0 / jnp.maximum(degree, 1.0)
    aggregate = summed * inverse[:, None]
    preactivation = jnp.dot(features, w_self, precision=HIGHEST) + jnp.dot(aggregate, w_neigh, precision=HIGHEST)
    gate_sigmoid = jax.nn.sigmoid(preactivation)
    hidden = preactivation * gate_sigmoid
    grad_pre = upstream * gate_sigmoid * (1.0 + preactivation * (1.0 - gate_sigmoid))
    grad_self = jnp.einsum("nf,ng->fg", features, grad_pre, precision=HIGHEST)
    grad_neigh = jnp.einsum("nf,ng->fg", aggregate, grad_pre, precision=HIGHEST)
    back_sum, _ = propagate(tile_coords, tile_count, tile_bits, grad_pre * inverse[:, None], True)
    grad_features = jnp.dot(grad_pre, w_self.T, precision=HIGHEST) + jnp.dot(back_sum, w_neigh.T, precision=HIGHEST)
    return hidden, grad_features, grad_self, grad_neigh
```

```python
import functools

import jax
import jax.numpy as jnp
from jax import lax
from jax.experimental import pallas as pl
from jax.experimental.pallas import tpu as pltpu
from jax.sharding import PartitionSpec as P

HIGH = lax.Precision.HIGH
UNROLL = 8
BLOCK = 128
DEGREE_ROWS = 8

SMEM = pl.BlockSpec(memory_space=pltpu.SMEM)
VMEM = pl.BlockSpec(memory_space=pltpu.VMEM)


def split_halves(value):
    high = value.astype(jnp.bfloat16)
    low = (value - high.astype(jnp.float32)).astype(jnp.bfloat16)
    return high, low


def unpack(words):
    shift = lax.broadcasted_iota(jnp.int32, (16, 8, BLOCK), 1)
    spread = jnp.broadcast_to(words[:, None, :], (16, 8, BLOCK))
    return ((spread >> shift) & 1).reshape(BLOCK, BLOCK).astype(jnp.float32)


def tile_loop(count_ref, coords_ref, bits_ref, visit):
    count = count_ref[0, 0]

    def step(group, carry):
        for offset in range(UNROLL):
            slot = group * UNROLL + offset
            mask = jnp.where(slot < count, 255, 0)
            tile = unpack(bits_ref[slot] & mask)
            visit(coords_ref[slot, 0], coords_ref[slot, 1], tile)
        return carry

    lax.fori_loop(0, (count + UNROLL - 1) // UNROLL, step, 0)


def forward_kernel(count_ref, coords_ref, bits_ref, x_ref, out_ref, pieces):
    feat = x_ref.shape[1]

    def prepare(shard, carry):
        for half in range(2):
            high, low = split_halves(x_ref[shard, :, half * BLOCK : (half + 1) * BLOCK])
            pieces[2 * shard + half, :, 0:BLOCK] = high
            pieces[2 * shard + half, :, BLOCK : 2 * BLOCK] = low
        return carry

    lax.fori_loop(0, x_ref.shape[0], prepare, 0)
    out_ref[...] = jnp.zeros_like(out_ref)

    def visit(i, j, tile):
        narrow = tile.astype(jnp.bfloat16)
        out_ref[i, 0:feat, :] += jnp.dot(
            pieces[j],
            jnp.concatenate([narrow, narrow], axis=0),
            preferred_element_type=jnp.float32,
        )
        out_ref[i, feat : feat + DEGREE_ROWS, :] += tile.reshape(16, 8, BLOCK).sum(0)

    tile_loop(count_ref, coords_ref, bits_ref, visit)


def backward_kernel(count_ref, coords_ref, bits_ref, g_ref, out_ref, pieces):
    def prepare(block, carry):
        high, low = split_halves(g_ref[block])
        pieces[block, 0:BLOCK, :] = high
        pieces[block, BLOCK : 2 * BLOCK, :] = low
        return carry

    lax.fori_loop(0, g_ref.shape[0], prepare, 0)
    out_ref[...] = jnp.zeros_like(out_ref)

    def visit(i, j, tile):
        narrow = tile.astype(jnp.bfloat16)
        out_ref[j] += jnp.dot(
            jnp.concatenate([narrow, narrow], axis=1),
            pieces[i],
            preferred_element_type=jnp.float32,
        )

    tile_loop(count_ref, coords_ref, bits_ref, visit)


def run_tiles(kernel, count, coords, bits, source, out_shape, name):
    feat_blocks = source.size // (BLOCK * 256)
    work = 2 * 2 * bits.shape[0] * BLOCK * BLOCK * 256
    return pl.pallas_call(
        kernel,
        out_shape=jax.ShapeDtypeStruct(out_shape, jnp.float32),
        in_specs=[SMEM, SMEM, VMEM, VMEM],
        out_specs=VMEM,
        scratch_shapes=[pltpu.VMEM((feat_blocks, 256, 256), jnp.bfloat16)],
        compiler_params=pltpu.CompilerParams(vmem_limit_bytes=40 * 2**20),
        cost_estimate=pl.CostEstimate(
            flops=work, bytes_accessed=10 * 2**20, transcendentals=0
        ),
        name=name,
    )(count, coords, bits, source)


def exchange(value, axis, size, stride):
    devices = lax.axis_size(axis)

    def partner(index, distance):
        digit = index // stride % size
        return index + ((digit + distance) % size - digit) * stride

    def send(piece, distance):
        pairs = [(index, partner(index, distance)) for index in range(devices)]
        return lax.ppermute(piece, axis, pairs)

    return lax.axis_index(axis) // stride % size, send


GROUPS = (("row", 2, 1), ("row", 2, 2), ("row", 4, 4), ("col", 4, 1), ("col", 4, 4))


def sum_everywhere(value):
    for axis, size, stride in GROUPS:
        digit, send = exchange(value, axis, size, stride)
        rows = value.shape[0] // size

        def part(which, value=value, rows=rows):
            return lax.dynamic_slice_in_dim(value, which * rows, rows, 0)

        total = part(digit)
        for distance in range(1, size):
            total = total + send(part((digit + distance) % size), distance)
        value = total
    for axis, size, stride in reversed(GROUPS):
        digit, send = exchange(value, axis, size, stride)
        rows = value.shape[0]
        whole = jnp.zeros((rows * size,) + value.shape[1:], value.dtype)
        whole = lax.dynamic_update_slice_in_dim(whole, value, digit * rows, 0)
        for distance in range(1, size):
            origin = (digit + size - distance) % size
            whole = lax.dynamic_update_slice_in_dim(
                whole, send(value, distance), origin * rows, 0
            )
        value = whole
    return value


def local(features, w_self, w_neigh, upstream, tile_coords, tile_count, tile_bits):
    devices = lax.axis_size("row")
    rows_dev, feat = features.shape
    blocks = rows_dev * devices // BLOCK
    coords, bits = tile_coords[0, 0], tile_bits[0, 0]
    swap = [
        (r * devices + c, c * devices + r) for r in range(devices) for c in range(devices)
    ]

    gathered = lax.all_gather(features.T, "row", axis=0, tiled=False)
    own = lax.ppermute(features, ("row", "col"), swap)
    sums = run_tiles(
        forward_kernel,
        tile_count,
        coords,
        bits,
        gathered,
        (blocks, feat + DEGREE_ROWS, BLOCK),
        "forward",
    )
    sums = lax.psum_scatter(sums, "col", scatter_dimension=0, tiled=True)
    degree = sums[:, feat:, :].sum(1)
    inverse = 1.0 / jnp.maximum(degree, 1.0)
    aggregate = (sums[:, :feat, :] * inverse[:, None, :]).swapaxes(1, 2)
    aggregate = aggregate.reshape(rows_dev, feat)
    inverse = inverse.reshape(rows_dev, 1)
    preact = jnp.dot(own, w_self, precision=HIGH) + jnp.dot(
        aggregate, w_neigh, precision=HIGH
    )
    gate = jax.nn.sigmoid(preact)
    hidden = preact * gate
    grad_pre = upstream * gate * (1.0 + preact * (1.0 - gate))

    grad_rows = lax.all_gather(grad_pre * inverse, "col", axis=0, tiled=True)
    grad_own = lax.ppermute(grad_pre, ("row", "col"), swap)
    weights = jnp.dot(
        jnp.concatenate([own, aggregate], axis=1).T, grad_pre, precision=HIGH
    )
    weights = sum_everywhere(weights)
    back = run_tiles(
        backward_kernel,
        tile_count,
        coords,
        bits,
        grad_rows.reshape(blocks, BLOCK, feat),
        (blocks, BLOCK, feat),
        "backward",
    )
    back = lax.psum_scatter(
        back.reshape(blocks * BLOCK, feat), "row", scatter_dimension=0, tiled=True
    )
    grad_features = jnp.dot(grad_own, w_self.T, precision=HIGH) + jnp.dot(
        back, w_neigh.T, precision=HIGH
    )
    return hidden, grad_features, weights[:feat], weights[feat:]


def solution(mesh):
    return jax.shard_map(
        local,
        mesh=mesh,
        in_specs=(
            P(("col", "row"), None),
            P(),
            P(),
            P(("row", "col"), None),
            P("row", "col", None, None),
            P("row", "col"),
            P("row", "col", None, None, None),
        ),
        out_specs=(P(("row", "col"), None), P(("col", "row"), None), P(), P()),
        check_vma=False,
    )
```

```python
import functools

import jax
import jax.numpy as jnp
from jax import lax
from jax.experimental import pallas as pl
from jax.experimental.pallas import tpu as pltpu
from jax.sharding import PartitionSpec as P

HIGH = lax.Precision.HIGH
UNROLL = 8
BLOCK = 128
SPLIT = 192
DEGREE_ROWS = 8
GATHER_BY_STEPS = False

SMEM = pl.BlockSpec(memory_space=pltpu.SMEM)
VMEM = pl.BlockSpec(memory_space=pltpu.VMEM)

CORE = ("row", 2, 1)
PAIR = ("row", 2, 2)
RING_Y = ("row", 4, 4)
RING_Z = ("col", 4, 1)
RING_X = ("col", 4, 4)


def split_halves(value):
    high = value.astype(jnp.bfloat16)
    low = (value - high.astype(jnp.float32)).astype(jnp.bfloat16)
    return high, low


def unpack(words):
    shift = lax.broadcasted_iota(jnp.int32, (16, 8, BLOCK), 1)
    spread = jnp.broadcast_to(words[:, None, :], (16, 8, BLOCK))
    return ((spread >> shift) & 1).reshape(BLOCK, BLOCK).astype(jnp.float32)


def tile_loop(count_ref, bits_ref, visit):
    count = count_ref[0, 0]

    def step(group, carry):
        for offset in range(UNROLL):
            slot = group * UNROLL + offset
            mask = jnp.where(slot < count, 255, 0)
            tile = unpack(bits_ref[slot] & mask)
            visit(slot, tile)
        return carry

    lax.fori_loop(0, (count + UNROLL - 1) // UNROLL, step, 0)


def forward_kernel(
    count_ref, first_ref, second_ref, source_ref, bits_ref, *refs
):
    *inputs, first_out, second_out, pieces = refs
    place = 0
    for x_ref in inputs:

        def prepare(block, carry, x_ref=x_ref, place=place):
            high, low = split_halves(x_ref[block])
            pieces[place + block, :, 0:BLOCK] = high
            pieces[place + block, :, BLOCK : 2 * BLOCK] = low
            return carry

        lax.fori_loop(0, x_ref.shape[0], prepare, 0)
        place += x_ref.shape[0]
    first_out[...] = jnp.zeros_like(first_out)
    second_out[...] = jnp.zeros_like(second_out)

    def visit(slot, tile):
        narrow = tile.astype(jnp.bfloat16)
        first, second = first_ref[slot], second_ref[slot]
        product = jnp.dot(
            pieces[source_ref[slot]],
            jnp.concatenate([narrow, narrow], axis=0),
            preferred_element_type=jnp.float32,
        )
        first_out[first, 0:SPLIT, :] += product[:SPLIT]
        second_out[second, :, :] += product[SPLIT:]
        first_out[first, SPLIT:, :] += tile.reshape(16, 8, BLOCK).sum(0)

    tile_loop(count_ref, bits_ref, visit)


def backward_kernel(count_ref, target_ref, source_ref, bits_ref, *refs):
    *inputs, out_ref, pieces = refs
    place = 0
    for g_ref in inputs:

        def prepare(block, carry, g_ref=g_ref, place=place):
            high, low = split_halves(g_ref[block])
            pieces[place + block, 0:BLOCK, :] = high
            pieces[place + block, BLOCK : 2 * BLOCK, :] = low
            return carry

        lax.fori_loop(0, g_ref.shape[0], prepare, 0)
        place += g_ref.shape[0]
    out_ref[...] = jnp.zeros_like(out_ref)

    def visit(slot, tile):
        narrow = tile.astype(jnp.bfloat16)
        out_ref[target_ref[slot]] += jnp.dot(
            jnp.concatenate([narrow, narrow], axis=1),
            pieces[source_ref[slot]],
            preferred_element_type=jnp.float32,
        )

    tile_loop(count_ref, bits_ref, visit)


def run_tiles(kernel, scalars, bits, inputs, out_rows, name):
    blocks = sum(piece.shape[0] for piece in inputs)
    work = 2 * 2 * bits.shape[0] * BLOCK * BLOCK * 256
    return pl.pallas_call(
        kernel,
        out_shape=tuple(
            jax.ShapeDtypeStruct((blocks,) + shape, jnp.float32) for shape in out_rows
        ),
        in_specs=[SMEM] * len(scalars) + [VMEM] * (1 + len(inputs)),
        out_specs=(VMEM,) * len(out_rows),
        scratch_shapes=[pltpu.VMEM((blocks, 256, 256), jnp.bfloat16)],
        compiler_params=pltpu.CompilerParams(vmem_limit_bytes=40 * 2**20),
        cost_estimate=pl.CostEstimate(
            flops=4 * work, bytes_accessed=10 * 2**20, transcendentals=0
        ),
        name=name,
    )(*scalars, bits, *inputs)


def digit_of(digit):
    axis, size, stride = digit
    return lax.axis_index(axis) // stride % size


def send(piece, digit, distance):
    axis, size, stride = digit
    pairs = []
    for index in range(lax.axis_size(axis)):
        own = index // stride % size
        pairs.append((index, index + ((own + distance) % size - own) * stride))
    return lax.ppermute(piece, axis, pairs)


def swap_gather(value, digit):
    return [value, send(value, digit, 1)]


def ring_gather(value, digit):
    half = value.shape[0] // 2
    before = send(value, digit, 1)
    after = send(value, digit, 3)
    far_first = send(before[:half], digit, 1)
    far_second = send(after[half:], digit, 3)
    return [value, after, far_first, far_second, before]


def ring_scatter(value, digit):
    half = value.shape[0] // 8
    near, up, far, down = (value[2 * half * k : 2 * half * (k + 1)] for k in range(4))
    first = send(far[:half], digit, 1)
    second = send(far[half:], digit, 3)
    up_second = send(up[half:], digit, 1)
    down_first = send(down[:half], digit, 3)
    up_first = send(up[:half] + first, digit, 1)
    down_second = send(down[half:] + second, digit, 3)
    return jnp.concatenate(
        [near[:half] + down_first + up_first, near[half:] + up_second + down_second]
    )


def ring_scatter_whole(value, digit):
    half = value.shape[0] // 8
    near, up, far, down = (value[2 * half * k : 2 * half * (k + 1)] for k in range(4))
    first = send(far[:half], digit, 1)
    second = send(far[half:], digit, 3)
    up = send(jnp.concatenate([up[:half] + first, up[half:]]), digit, 1)
    down = send(jnp.concatenate([down[:half], down[half:] + second]), digit, 3)
    return near + up + down


def swap_scatter(value, digit):
    half = value.shape[0] // 2
    return value[:half] + send(value[half:], digit, 1)


def gather_row(value):
    near = jnp.concatenate(ring_gather(value, RING_Y))
    far = jnp.concatenate(ring_gather(send(value, PAIR, 1), RING_Y))
    return swap_gather(near, CORE) + swap_gather(far, CORE)


def gather_row_place(block):
    shard = block // 2
    place = relative(PAIR, shard) * 2 + relative(CORE, shard)
    return (place * 4 + relative(RING_Y, shard)) * 2 + block % 2


def scatter_row(value):
    return swap_scatter(ring_scatter(swap_scatter(value, CORE), RING_Y), PAIR)


def scatter_row_place(block):
    shard = block // 2
    place = relative(CORE, shard) * 4 + relative(RING_Y, shard)
    return (place * 2 + relative(PAIR, shard)) * 2 + block % 2


def gather_col(value):
    own, after, far_first, far_second, before = ring_gather(value, RING_Z)
    far = jnp.concatenate([far_first, far_second])
    pieces = []
    for piece in (own, after, before, far):
        pieces += ring_gather(piece, RING_X)
    return pieces


def gather_col_place(block):
    shard = block // 2
    along = relative(RING_Z, shard)
    return ((along ^ (along >> 1)) * 4 + relative(RING_X, shard)) * 2 + block % 2


def scatter_col(value, digits):
    for digit in digits:
        value = ring_scatter_whole(value, digit)
    return value


def scatter_col_place(block, digits):
    shard = block // 2
    place = relative(digits[0], shard) * 4 + relative(digits[1], shard)
    return place * 2 + block % 2


def relative(digit, number):
    _, size, stride = digit
    return (number // stride % size - digit_of(digit)) % size


def sum_everywhere(value):
    for group in (CORE, PAIR, RING_Y):
        size, digit = group[1], digit_of(group)
        rows = value.shape[0] // size

        def part(distance, value=value, rows=rows, digit=digit, size=size):
            start = (digit + distance) % size * rows
            return lax.dynamic_slice_in_dim(value, start, rows, 0)

        parts = [part(0)] + [
            send(part(distance), group, distance) for distance in range(1, size)
        ]
        value = sum(parts[1:], parts[0])
    for group in (RING_Z, RING_X):
        one, two, three = (send(value, group, distance) for distance in (1, 2, 3))
        value = (value + two) + (one + three)
    for group in (RING_Y, PAIR, CORE):
        size, digit = group[1], digit_of(group)
        pieces = [value] + [send(value, group, size - d) for d in range(1, size)]
        pieces = jnp.concatenate(pieces + pieces)
        rows = value.shape[0]
        start = (size - digit) % size * rows
        value = lax.dynamic_slice_in_dim(pieces, start, rows * size, 0)
    return value


def local(features, w_self, w_neigh, upstream, tile_coords, tile_count, tile_bits):
    devices = lax.axis_size("row")
    rows_dev, feat = features.shape
    per_dev = rows_dev // BLOCK
    bits = tile_bits[0, 0]
    row_block, col_block = tile_coords[0, 0, :, 0], tile_coords[0, 0, :, 1]
    swap = [
        (r * devices + c, c * devices + r) for r in range(devices) for c in range(devices)
    ]

    turned = features.reshape(per_dev, BLOCK, feat).swapaxes(1, 2)
    gathered = gather_row(turned)
    first, second = run_tiles(
        forward_kernel,
        (
            tile_count,
            scatter_col_place(row_block, (RING_X, RING_Z)),
            scatter_col_place(row_block, (RING_Z, RING_X)),
            gather_row_place(col_block),
        ),
        bits,
        gathered,
        ((SPLIT + DEGREE_ROWS, BLOCK), (feat - SPLIT, BLOCK)),
        "forward",
    )
    own = lax.ppermute(features, ("row", "col"), swap)
    first = scatter_col(first, (RING_X, RING_Z))
    second = scatter_col(second, (RING_Z, RING_X))

    degree = first[:, SPLIT:, :].sum(1)
    inverse = 1.0 / jnp.maximum(degree, 1.0)
    total = jnp.concatenate([first[:, :SPLIT], second], axis=1)
    aggregate = (total * inverse[:, None, :]).swapaxes(1, 2).reshape(rows_dev, feat)
    inverse = inverse.reshape(rows_dev, 1)
    preact = jnp.dot(own, w_self, precision=HIGH) + jnp.dot(
        aggregate, w_neigh, precision=HIGH
    )
    gate = jax.nn.sigmoid(preact)
    hidden = preact * gate
    grad_pre = upstream * gate * (1.0 + preact * (1.0 - gate))

    scaled = grad_pre * inverse
    if GATHER_BY_STEPS:
        gathered = gather_col(scaled.reshape(per_dev, BLOCK, feat))
        source = gather_col_place(row_block)
    else:
        gathered = lax.all_gather(scaled, "col", axis=0, tiled=True)
        gathered = [gathered.reshape(devices * per_dev, BLOCK, feat)]
        source = row_block
    weights = jnp.dot(
        jnp.concatenate([own, aggregate], axis=1).T, grad_pre, precision=HIGH
    )
    weights = sum_everywhere(weights)
    grad_own = lax.ppermute(grad_pre, ("row", "col"), swap)
    if not GATHER_BY_STEPS:
        gathered[0], weights, grad_own = lax.optimization_barrier(
            (gathered[0], weights, grad_own)
        )
    (back,) = run_tiles(
        backward_kernel,
        (tile_count, scatter_row_place(col_block), source),
        bits,
        gathered,
        ((BLOCK, feat),),
        "backward",
    )
    back = scatter_row(back).reshape(rows_dev, feat)
    grad_features = jnp.dot(grad_own, w_self.T, precision=HIGH) + jnp.dot(
        back, w_neigh.T, precision=HIGH
    )
    return hidden, grad_features, weights[:feat], weights[feat:]


def solution(mesh):
    return jax.shard_map(
        local,
        mesh=mesh,
        in_specs=(
            P(("col", "row"), None),
            P(),
            P(),
            P(("row", "col"), None),
            P("row", "col", None, None),
            P("row", "col"),
            P("row", "col", None, None, None),
        ),
        out_specs=(P(("row", "col"), None), P(("col", "row"), None), P(), P()),
        check_vma=False,
    )
```

```python
import functools

import jax
import jax.numpy as jnp
from jax import lax
from jax.experimental import pallas as pl
from jax.experimental.pallas import tpu as pltpu
from jax.sharding import PartitionSpec as P

HIGH = lax.Precision.HIGH
UNROLL = 8
BLOCK = 128
SPLIT = 192
DEGREE_ROWS = 8

SMEM = pl.BlockSpec(memory_space=pltpu.SMEM)
VMEM = pl.BlockSpec(memory_space=pltpu.VMEM)
ANY = pl.BlockSpec(memory_space=pl.ANY)

CORE = ("row", 2, 1)
PAIR = ("row", 2, 2)
RING_Y = ("row", 4, 4)
RING_Z = ("col", 4, 1)
RING_X = ("col", 4, 4)


def split_halves(value):
    high = value.astype(jnp.bfloat16)
    low = (value - high.astype(jnp.float32)).astype(jnp.bfloat16)
    return high, low


def unpack(words):
    shift = lax.broadcasted_iota(jnp.int32, (16, 8, BLOCK), 1)
    spread = jnp.broadcast_to(words[:, None, :], (16, 8, BLOCK))
    return ((spread >> shift) & 1).reshape(BLOCK, BLOCK).astype(jnp.float32)


def tile_loop(count_ref, bits_ref, visit):
    count = count_ref[0, 0]

    def step(group, carry):
        for offset in range(UNROLL):
            slot = group * UNROLL + offset
            mask = jnp.where(slot < count, 255, 0)
            tile = unpack(bits_ref[slot] & mask)
            visit(slot, tile)
        return carry

    lax.fori_loop(0, (count + UNROLL - 1) // UNROLL, step, 0)


def bring(inputs, stage, sems, clear, prepare):
    copies, place = [], 0
    for number, ref in enumerate(inputs):
        blocks = ref.shape[0]
        copies.append(
            pltpu.make_async_copy(ref, stage.at[place : place + blocks], sems.at[number])
        )
        copies[-1].start()
        place += blocks
    clear()
    place = 0
    for copy, ref in zip(copies, inputs):
        copy.wait()
        lax.fori_loop(place, place + ref.shape[0], prepare, 0)
        place += ref.shape[0]


def forward_kernel(
    count_ref, first_ref, second_ref, source_ref, bits_ref, *refs
):
    *inputs, first_out, second_out, pieces, stage, sems = refs

    def clear():
        first_out[...] = jnp.zeros_like(first_out)
        second_out[...] = jnp.zeros_like(second_out)

    def prepare(block, carry):
        high, low = split_halves(stage[block])
        pieces[block, :, 0:BLOCK] = high
        pieces[block, :, BLOCK : 2 * BLOCK] = low
        return carry

    bring(inputs, stage, sems, clear, prepare)

    def visit(slot, tile):
        narrow = tile.astype(jnp.bfloat16)
        first, second = first_ref[slot], second_ref[slot]
        product = jnp.dot(
            pieces[source_ref[slot]],
            jnp.concatenate([narrow, narrow], axis=0),
            preferred_element_type=jnp.float32,
        )
        first_out[first, 0:SPLIT, :] += product[:SPLIT]
        second_out[second, :, :] += product[SPLIT:]
        first_out[first, SPLIT:, :] += tile.reshape(16, 8, BLOCK).sum(0)

    tile_loop(count_ref, bits_ref, visit)


def backward_kernel(count_ref, target_ref, source_ref, bits_ref, *refs):
    *inputs, out_ref, pieces, stage, sems = refs

    def clear():
        out_ref[...] = jnp.zeros_like(out_ref)

    def prepare(block, carry):
        high, low = split_halves(stage[block])
        pieces[block, 0:BLOCK, :] = high
        pieces[block, BLOCK : 2 * BLOCK, :] = low
        return carry

    bring(inputs, stage, sems, clear, prepare)

    def visit(slot, tile):
        narrow = tile.astype(jnp.bfloat16)
        out_ref[target_ref[slot]] += jnp.dot(
            jnp.concatenate([narrow, narrow], axis=1),
            pieces[source_ref[slot]],
            preferred_element_type=jnp.float32,
        )

    tile_loop(count_ref, bits_ref, visit)


def run_tiles(kernel, scalars, bits, inputs, out_rows, name):
    blocks = sum(piece.shape[0] for piece in inputs)
    work = 2 * 2 * bits.shape[0] * BLOCK * BLOCK * 256
    return pl.pallas_call(
        kernel,
        out_shape=tuple(
            jax.ShapeDtypeStruct((blocks,) + shape, jnp.float32) for shape in out_rows
        ),
        in_specs=[SMEM] * len(scalars) + [VMEM] + [ANY] * len(inputs),
        out_specs=(VMEM,) * len(out_rows),
        scratch_shapes=[
            pltpu.VMEM((blocks, 256, 256), jnp.bfloat16),
            pltpu.VMEM((blocks,) + inputs[0].shape[1:], jnp.float32),
            pltpu.SemaphoreType.DMA((len(inputs),)),
        ],
        compiler_params=pltpu.CompilerParams(vmem_limit_bytes=40 * 2**20),
        cost_estimate=pl.CostEstimate(
            flops=4 * work, bytes_accessed=10 * 2**20, transcendentals=0
        ),
        name=name,
    )(*scalars, bits, *inputs)


def digit_of(digit):
    axis, size, stride = digit
    return lax.axis_index(axis) // stride % size


def send(piece, digit, distance):
    axis, size, stride = digit
    pairs = []
    for index in range(lax.axis_size(axis)):
        own = index // stride % size
        pairs.append((index, index + ((own + distance) % size - own) * stride))
    return lax.ppermute(piece, axis, pairs)


def swap_gather(value, digit):
    return [value, send(value, digit, 1)]


def ring_gather(value, digit):
    half = value.shape[0] // 2
    before = send(value, digit, 1)
    after = send(value, digit, 3)
    far_first = send(before[:half], digit, 1)
    far_second = send(after[half:], digit, 3)
    return [value, after, far_first, far_second, before]


def quarters(value):
    rows = value.shape[0] // 4
    return (value[rows * k : rows * (k + 1)] for k in range(4))


def scatter_far(value, digit):
    _, _, far, _ = quarters(value)
    half = far.shape[0] // 2
    return send(far[:half], digit, 1), send(far[half:], digit, 3)


def scatter_near(value, digit, arrived):
    near, up, _, down = quarters(value)
    first, second = arrived
    half = near.shape[0] // 2
    up = send(jnp.concatenate([up[:half] + first, up[half:]]), digit, 1)
    down = send(jnp.concatenate([down[:half], down[half:] + second]), digit, 3)
    return near + up + down


def swap_scatter(value, digit):
    half = value.shape[0] // 2
    return value[:half] + send(value[half:], digit, 1)


def gather_row(value):
    near = jnp.concatenate(ring_gather(value, RING_Y))
    far = jnp.concatenate(ring_gather(send(value, PAIR, 1), RING_Y))
    return swap_gather(near, CORE) + swap_gather(far, CORE)


def gather_row_place(block):
    shard = block // 2
    place = relative(PAIR, shard) * 2 + relative(CORE, shard)
    return (place * 4 + relative(RING_Y, shard)) * 2 + block % 2


def scatter_row_place(block):
    shard = block // 2
    place = relative(CORE, shard) * 4 + relative(RING_Y, shard)
    return (place * 2 + relative(PAIR, shard)) * 2 + block % 2


def gather_col(value):
    own, after, far_first, far_second, before = ring_gather(value, RING_Z)
    far = jnp.concatenate([far_first, far_second])
    pieces = []
    for piece in (own, after, before, far):
        pieces += ring_gather(piece, RING_X)
    return pieces


def gather_col_place(block):
    shard = block // 2
    along = relative(RING_Z, shard)
    return ((along ^ (along >> 1)) * 4 + relative(RING_X, shard)) * 2 + block % 2


def scatter_col(first, second):
    for one, two in ((RING_X, RING_Z), (RING_Z, RING_X)):
        far = lax.optimization_barrier(
            (scatter_far(first, one), scatter_far(second, two))
        )
        first, second = lax.optimization_barrier(
            (scatter_near(first, one, far[0]), scatter_near(second, two, far[1]))
        )
    return first, second


def scatter_col_place(block, digits):
    shard = block // 2
    place = relative(digits[0], shard) * 4 + relative(digits[1], shard)
    return place * 2 + block % 2


def relative(digit, number):
    _, size, stride = digit
    return (number // stride % size - digit_of(digit)) % size


def sum_parts(value, groups):
    for group in groups:
        size, digit = group[1], digit_of(group)
        rows = value.shape[0] // size

        def part(distance, value=value, rows=rows, digit=digit, size=size):
            start = (digit + distance) % size * rows
            return lax.dynamic_slice_in_dim(value, start, rows, 0)

        parts = [part(0)] + [
            send(part(distance), group, distance) for distance in range(1, size)
        ]
        value = sum(parts[1:], parts[0])
    return value


def sum_ring(value, digit):
    one, two, three = (send(value, digit, distance) for distance in (1, 2, 3))
    return (value + two) + (one + three)


def gather_ring(value, digit):
    size, own = digit[1], digit_of(digit)
    pieces = [value] + [send(value, digit, size - d) for d in range(1, size)]
    pieces = jnp.concatenate(pieces + pieces)
    rows = value.shape[0]
    return lax.dynamic_slice_in_dim(pieces, (size - own) % size * rows, rows * size, 0)


def scatter_row(value, weights):
    value = swap_scatter(value, CORE)
    value, weights = lax.optimization_barrier((value, weights))
    far, weights = lax.optimization_barrier(
        (scatter_far(value, RING_Y), sum_ring(weights, RING_Z))
    )
    value, weights = lax.optimization_barrier(
        (scatter_near(value, RING_Y, far), sum_ring(weights, RING_X))
    )
    value, weights = swap_scatter(value, PAIR), gather_ring(weights, RING_Y)
    return value, gather_ring(gather_ring(weights, PAIR), CORE)


def local(features, w_self, w_neigh, upstream, tile_coords, tile_count, tile_bits):
    devices = lax.axis_size("row")
    rows_dev, feat = features.shape
    per_dev = rows_dev // BLOCK
    bits = tile_bits[0, 0]
    row_block, col_block = tile_coords[0, 0, :, 0], tile_coords[0, 0, :, 1]
    swap = [
        (r * devices + c, c * devices + r) for r in range(devices) for c in range(devices)
    ]

    turned = features.reshape(per_dev, BLOCK, feat).swapaxes(1, 2)
    gathered = gather_row(turned)
    first, second = run_tiles(
        forward_kernel,
        (
            tile_count,
            scatter_col_place(row_block, (RING_X, RING_Z)),
            scatter_col_place(row_block, (RING_Z, RING_X)),
            gather_row_place(col_block),
        ),
        bits,
        gathered,
        ((SPLIT + DEGREE_ROWS, BLOCK), (feat - SPLIT, BLOCK)),
        "forward",
    )
    own = lax.ppermute(features, ("row", "col"), swap)
    first, second, own = lax.optimization_barrier((first, second, own))
    first, second = scatter_col(first, second)

    degree = first[:, SPLIT:, :].sum(1)
    inverse = 1.0 / jnp.maximum(degree, 1.0)
    total = jnp.concatenate([first[:, :SPLIT], second], axis=1)
    aggregate = (total * inverse[:, None, :]).swapaxes(1, 2).reshape(rows_dev, feat)
    inverse = inverse.reshape(rows_dev, 1)
    preact = jnp.dot(own, w_self, precision=HIGH) + jnp.dot(
        aggregate, w_neigh, precision=HIGH
    )
    gate = jax.nn.sigmoid(preact)
    hidden = preact * gate
    grad_pre = upstream * gate * (1.0 + preact * (1.0 - gate))

    scaled = grad_pre * inverse
    weights = jnp.dot(
        jnp.concatenate([own, aggregate], axis=1).T, grad_pre, precision=HIGH
    )
    scaled, weights = lax.optimization_barrier((scaled, weights))
    weights = sum_parts(weights, (CORE, PAIR, RING_Y))
    gathered = gather_col(scaled.reshape(per_dev, BLOCK, feat))
    gathered, weights = lax.optimization_barrier((gathered, weights))
    grad_own = lax.ppermute(grad_pre, ("row", "col"), swap)
    (back,) = run_tiles(
        backward_kernel,
        (tile_count, scatter_row_place(col_block), gather_col_place(row_block)),
        bits,
        gathered,
        ((BLOCK, feat),),
        "backward",
    )
    back, grad_own = lax.optimization_barrier((back, grad_own))
    back, weights = scatter_row(back, weights)
    back = back.reshape(rows_dev, feat)
    grad_features = jnp.dot(grad_own, w_self.T, precision=HIGH) + jnp.dot(
        back, w_neigh.T, precision=HIGH
    )
    return hidden, grad_features, weights[:feat], weights[feat:]


def solution(mesh):
    return jax.shard_map(
        local,
        mesh=mesh,
        in_specs=(
            P(("col", "row"), None),
            P(),
            P(),
            P(("row", "col"), None),
            P("row", "col", None, None),
            P("row", "col"),
            P("row", "col", None, None, None),
        ),
        out_specs=(P(("row", "col"), None), P(("col", "row"), None), P(), P()),
        check_vma=False,
    )
```

```python
import functools

import jax
import jax.numpy as jnp
from jax import lax
from jax.experimental import pallas as pl
from jax.experimental.pallas import tpu as pltpu
from jax.sharding import PartitionSpec as P

HIGH = lax.Precision.HIGH
UNROLL = 16
BLOCK = 128
SPLIT = 192
DEGREE_ROWS = 8

SMEM = pl.BlockSpec(memory_space=pltpu.SMEM)
VMEM = pl.BlockSpec(memory_space=pltpu.VMEM)
ANY = pl.BlockSpec(memory_space=pl.ANY)

CORE = ("row", 2, 1)
PAIR = ("row", 2, 2)
RING_Y = ("row", 4, 4)
RING_Z = ("col", 4, 1)
RING_X = ("col", 4, 4)


def split_halves(value):
    high = value.astype(jnp.bfloat16)
    low = (value - high.astype(jnp.float32)).astype(jnp.bfloat16)
    return high, low


def unpack(words):
    shift = lax.broadcasted_iota(jnp.int32, (16, 8, BLOCK), 1)
    spread = jnp.broadcast_to(words[:, None, :], (16, 8, BLOCK))
    return ((spread >> shift) & 1).reshape(BLOCK, BLOCK).astype(jnp.float32)


def tile_loop(count_ref, bits_ref, visit):
    count = count_ref[0, 0]

    def step(group, carry):
        for offset in range(UNROLL):
            slot = group * UNROLL + offset
            mask = jnp.where(slot < count, 255, 0)
            tile = unpack(bits_ref[slot] & mask)
            visit(slot, tile)
        return carry

    lax.fori_loop(0, (count + UNROLL - 1) // UNROLL, step, 0)


def bring(inputs, stage, sems, clear, prepare):
    copies, place = [], 0
    for number, ref in enumerate(inputs):
        blocks = ref.shape[0]
        copies.append(
            pltpu.make_async_copy(ref, stage.at[place : place + blocks], sems.at[number])
        )
        copies[-1].start()
        place += blocks
    clear()
    place = 0
    for copy, ref in zip(copies, inputs):
        copy.wait()
        lax.fori_loop(place, place + ref.shape[0], prepare, 0)
        place += ref.shape[0]


def forward_kernel(
    count_ref, first_ref, second_ref, source_ref, bits_ref, *refs
):
    *inputs, first_out, second_out, pieces, stage, sems = refs

    def clear():
        first_out[...] = jnp.zeros_like(first_out)
        second_out[...] = jnp.zeros_like(second_out)

    def prepare(block, carry):
        high, low = split_halves(stage[block])
        pieces[block, :, 0:BLOCK] = high
        pieces[block, :, BLOCK : 2 * BLOCK] = low
        return carry

    bring(inputs, stage, sems, clear, prepare)

    def visit(slot, tile):
        narrow = tile.astype(jnp.bfloat16)
        first, second = first_ref[slot], second_ref[slot]
        product = jnp.dot(
            pieces[source_ref[slot]],
            jnp.concatenate([narrow, narrow], axis=0),
            preferred_element_type=jnp.float32,
        )
        first_out[first, 0:SPLIT, :] += product[:SPLIT]
        second_out[second, :, :] += product[SPLIT:]
        first_out[first, SPLIT:, :] += tile.reshape(16, 8, BLOCK).sum(0)

    tile_loop(count_ref, bits_ref, visit)


def backward_kernel(count_ref, target_ref, source_ref, bits_ref, *refs):
    *inputs, out_ref, pieces, stage, sems = refs

    def clear():
        out_ref[...] = jnp.zeros_like(out_ref)

    def prepare(block, carry):
        high, low = split_halves(stage[block])
        pieces[block, 0:BLOCK, :] = high
        pieces[block, BLOCK : 2 * BLOCK, :] = low
        return carry

    bring(inputs, stage, sems, clear, prepare)

    def visit(slot, tile):
        narrow = tile.astype(jnp.bfloat16)
        out_ref[target_ref[slot]] += jnp.dot(
            jnp.concatenate([narrow, narrow], axis=1),
            pieces[source_ref[slot]],
            preferred_element_type=jnp.float32,
        )

    tile_loop(count_ref, bits_ref, visit)


def run_tiles(kernel, scalars, bits, inputs, out_rows, name):
    blocks = sum(piece.shape[0] for piece in inputs)
    work = 2 * 2 * bits.shape[0] * BLOCK * BLOCK * 256
    return pl.pallas_call(
        kernel,
        out_shape=tuple(
            jax.ShapeDtypeStruct((blocks,) + shape, jnp.float32) for shape in out_rows
        ),
        in_specs=[SMEM] * len(scalars) + [VMEM] + [ANY] * len(inputs),
        out_specs=(VMEM,) * len(out_rows),
        scratch_shapes=[
            pltpu.VMEM((blocks, 256, 256), jnp.bfloat16),
            pltpu.VMEM((blocks,) + inputs[0].shape[1:], jnp.float32),
            pltpu.SemaphoreType.DMA((len(inputs),)),
        ],
        compiler_params=pltpu.CompilerParams(vmem_limit_bytes=40 * 2**20),
        cost_estimate=pl.CostEstimate(
            flops=4 * work, bytes_accessed=10 * 2**20, transcendentals=0
        ),
        name=name,
    )(*scalars, bits, *inputs)


def digit_of(digit):
    axis, size, stride = digit
    return lax.axis_index(axis) // stride % size


def send(piece, digit, distance):
    axis, size, stride = digit
    pairs = []
    for index in range(lax.axis_size(axis)):
        own = index // stride % size
        pairs.append((index, index + ((own + distance) % size - own) * stride))
    return lax.ppermute(piece, axis, pairs)


def swap_gather(value, digit):
    return [value, send(value, digit, 1)]


def ring_gather(value, digit):
    half = value.shape[0] // 2
    before = send(value, digit, 1)
    after = send(value, digit, 3)
    far_first = send(before[:half], digit, 1)
    far_second = send(after[half:], digit, 3)
    return [value, after, far_first, far_second, before]


def quarters(value):
    rows = value.shape[0] // 4
    return (value[rows * k : rows * (k + 1)] for k in range(4))


def scatter_far(value, digit):
    _, _, far, _ = quarters(value)
    half = far.shape[0] // 2
    return send(far[:half], digit, 1), send(far[half:], digit, 3)


def scatter_near(value, digit, arrived):
    near, up, _, down = quarters(value)
    first, second = arrived
    half = near.shape[0] // 2
    up = send(jnp.concatenate([up[:half] + first, up[half:]]), digit, 1)
    down = send(jnp.concatenate([down[:half], down[half:] + second]), digit, 3)
    return near + up + down


def swap_scatter(value, digit):
    half = value.shape[0] // 2
    return value[:half] + send(value[half:], digit, 1)


def gather_row(value):
    near = jnp.concatenate(ring_gather(value, RING_Y))
    far = jnp.concatenate(ring_gather(send(value, PAIR, 1), RING_Y))
    return swap_gather(near, CORE) + swap_gather(far, CORE)


def gather_row_place(block):
    shard = block // 2
    place = relative(PAIR, shard) * 2 + relative(CORE, shard)
    return (place * 4 + relative(RING_Y, shard)) * 2 + block % 2


def scatter_row_place(block):
    shard = block // 2
    place = relative(CORE, shard) * 4 + relative(RING_Y, shard)
    return (place * 2 + relative(PAIR, shard)) * 2 + block % 2


def gather_col(value):
    own, after, far_first, far_second, before = ring_gather(value, RING_Z)
    far = jnp.concatenate([far_first, far_second])
    pieces = []
    for piece in (own, jnp.concatenate([after, before]), far):
        pieces += ring_gather(piece, RING_X)
    return pieces


def gather_col_place(block):
    shard = block // 2
    along, across = relative(RING_Z, shard), relative(RING_X, shard)
    single = jnp.where(along == 0, 0, 12) + across
    double = 4 + across * 2 + along // 2
    return jnp.where(along % 2 == 1, double, single) * 2 + block % 2


def scatter_col(first, second):
    for one, two in ((RING_X, RING_Z), (RING_Z, RING_X)):
        far = lax.optimization_barrier(
            (scatter_far(first, one), scatter_far(second, two))
        )
        first, second = lax.optimization_barrier(
            (scatter_near(first, one, far[0]), scatter_near(second, two, far[1]))
        )
    return first, second


def scatter_col_place(block, digits):
    shard = block // 2
    place = relative(digits[0], shard) * 4 + relative(digits[1], shard)
    return place * 2 + block % 2


def relative(digit, number):
    _, size, stride = digit
    return (number // stride % size - digit_of(digit)) % size


def sum_parts(value, groups):
    for group in groups:
        size, digit = group[1], digit_of(group)
        rows = value.shape[0] // size

        def part(distance, value=value, rows=rows, digit=digit, size=size):
            start = (digit + distance) % size * rows
            return lax.dynamic_slice_in_dim(value, start, rows, 0)

        parts = [part(0)] + [
            send(part(distance), group, distance) for distance in range(1, size)
        ]
        value = sum(parts[1:], parts[0])
    return value


def sum_ring(value, digit):
    one, two, three = (send(value, digit, distance) for distance in (1, 2, 3))
    return (value + two) + (one + three)


def gather_ring(value, digit):
    size, own = digit[1], digit_of(digit)
    pieces = [value] + [send(value, digit, size - d) for d in range(1, size)]
    pieces = jnp.concatenate(pieces + pieces)
    rows = value.shape[0]
    return lax.dynamic_slice_in_dim(pieces, (size - own) % size * rows, rows * size, 0)


def scatter_row(value, weights):
    value = swap_scatter(value, CORE)
    value, weights = lax.optimization_barrier((value, weights))
    far, weights = lax.optimization_barrier(
        (scatter_far(value, RING_Y), sum_ring(weights, RING_Z))
    )
    value, weights = lax.optimization_barrier(
        (scatter_near(value, RING_Y, far), sum_ring(weights, RING_X))
    )
    value, weights = swap_scatter(value, PAIR), gather_ring(weights, RING_Y)
    return value, gather_ring(gather_ring(weights, PAIR), CORE)


def local(features, w_self, w_neigh, upstream, tile_coords, tile_count, tile_bits):
    devices = lax.axis_size("row")
    rows_dev, feat = features.shape
    per_dev = rows_dev // BLOCK
    bits = tile_bits[0, 0]
    row_block, col_block = tile_coords[0, 0, :, 0], tile_coords[0, 0, :, 1]
    swap = [
        (r * devices + c, c * devices + r) for r in range(devices) for c in range(devices)
    ]

    turned = features.reshape(per_dev, BLOCK, feat).swapaxes(1, 2)
    gathered = gather_row(turned)
    first, second = run_tiles(
        forward_kernel,
        (
            tile_count,
            scatter_col_place(row_block, (RING_X, RING_Z)),
            scatter_col_place(row_block, (RING_Z, RING_X)),
            gather_row_place(col_block),
        ),
        bits,
        gathered,
        ((SPLIT + DEGREE_ROWS, BLOCK), (feat - SPLIT, BLOCK)),
        "forward",
    )
    own = lax.ppermute(features, ("row", "col"), swap)
    first, second, own = lax.optimization_barrier((first, second, own))
    first, second = scatter_col(first, second)

    degree = first[:, SPLIT:, :].sum(1)
    inverse = 1.0 / jnp.maximum(degree, 1.0)
    total = jnp.concatenate([first[:, :SPLIT], second], axis=1)
    aggregate = (total * inverse[:, None, :]).swapaxes(1, 2).reshape(rows_dev, feat)
    inverse = inverse.reshape(rows_dev, 1)
    preact = jnp.dot(own, w_self, precision=HIGH) + jnp.dot(
        aggregate, w_neigh, precision=HIGH
    )
    gate = jax.nn.sigmoid(preact)
    hidden = preact * gate
    grad_pre = upstream * gate * (1.0 + preact * (1.0 - gate))

    scaled = grad_pre * inverse
    weights = jnp.dot(
        jnp.concatenate([own, aggregate], axis=1).T, grad_pre, precision=HIGH
    )
    scaled, weights = lax.optimization_barrier((scaled, weights))
    weights = sum_parts(weights, (CORE, PAIR, RING_Y))
    gathered = gather_col(scaled.reshape(per_dev, BLOCK, feat))
    gathered, weights = lax.optimization_barrier((gathered, weights))
    grad_own = lax.ppermute(grad_pre, ("row", "col"), swap)
    (back,) = run_tiles(
        backward_kernel,
        (tile_count, scatter_row_place(col_block), gather_col_place(row_block)),
        bits,
        gathered,
        ((BLOCK, feat),),
        "backward",
    )
    back, grad_own = lax.optimization_barrier((back, grad_own))
    back, weights = scatter_row(back, weights)
    back = back.reshape(rows_dev, feat)
    grad_features = jnp.dot(grad_own, w_self.T, precision=HIGH) + jnp.dot(
        back, w_neigh.T, precision=HIGH
    )
    return hidden, grad_features, weights[:feat], weights[feat:]


def solution(mesh):
    return jax.shard_map(
        local,
        mesh=mesh,
        in_specs=(
            P(("col", "row"), None),
            P(),
            P(),
            P(("row", "col"), None),
            P("row", "col", None, None),
            P("row", "col"),
            P("row", "col", None, None, None),
        ),
        out_specs=(P(("row", "col"), None), P(("col", "row"), None), P(), P()),
        check_vma=False,
    )
```

```python
import functools

import jax
import jax.numpy as jnp
from jax import lax
from jax.experimental import pallas as pl
from jax.experimental.pallas import tpu as pltpu
from jax.sharding import PartitionSpec as P

HIGH = lax.Precision.HIGH
UNROLL = 16
BLOCK = 128
SPLIT = 192
DEGREE_ROWS = 8

SMEM = pl.BlockSpec(memory_space=pltpu.SMEM)
VMEM = pl.BlockSpec(memory_space=pltpu.VMEM)
ANY = pl.BlockSpec(memory_space=pl.ANY)

CORE = ("row", 2, 1)
PAIR = ("row", 2, 2)
RING_Y = ("row", 4, 4)
RING_Z = ("col", 4, 1)
RING_X = ("col", 4, 4)


def split_halves(value):
    high = value.astype(jnp.bfloat16)
    low = (value - high.astype(jnp.float32)).astype(jnp.bfloat16)
    return high, low


def unpack(words):
    shift = lax.broadcasted_iota(jnp.int32, (16, 8, BLOCK), 1)
    spread = jnp.broadcast_to(words[:, None, :], (16, 8, BLOCK))
    return ((spread >> shift) & 1).reshape(BLOCK, BLOCK).astype(jnp.float32)


def tile_loop(count_ref, bits_ref, visit):
    count = count_ref[0, 0]

    def step(group, carry):
        for offset in range(UNROLL):
            slot = group * UNROLL + offset
            mask = jnp.where(slot < count, 255, 0)
            tile = unpack(bits_ref[slot] & mask)
            visit(slot, tile)
        return carry

    lax.fori_loop(0, (count + UNROLL - 1) // UNROLL, step, 0)


def bring(inputs, stage, bits_ref, words, sems, clear, prepare):
    copies, place = [], 0
    for number, ref in enumerate(inputs):
        blocks = ref.shape[0]
        copies.append(
            pltpu.make_async_copy(ref, stage.at[place : place + blocks], sems.at[number])
        )
        copies[-1].start()
        place += blocks
    bits = pltpu.make_async_copy(bits_ref, words, sems.at[len(inputs)])
    bits.start()
    clear()
    place = 0
    for copy, ref in zip(copies, inputs):
        copy.wait()
        lax.fori_loop(place, place + ref.shape[0], prepare, 0)
        place += ref.shape[0]
    bits.wait()


def forward_kernel(
    count_ref, first_ref, second_ref, source_ref, bits_ref, *refs
):
    *inputs, first_out, second_out, pieces, stage, words, sems = refs

    def clear():
        first_out[...] = jnp.zeros_like(first_out)
        second_out[...] = jnp.zeros_like(second_out)

    def prepare(block, carry):
        high, low = split_halves(stage[block])
        pieces[block, :, 0:BLOCK] = high
        pieces[block, :, BLOCK : 2 * BLOCK] = low
        return carry

    bring(inputs, stage, bits_ref, words, sems, clear, prepare)

    def visit(slot, tile):
        narrow = tile.astype(jnp.bfloat16)
        first, second = first_ref[slot], second_ref[slot]
        product = jnp.dot(
            pieces[source_ref[slot]],
            jnp.concatenate([narrow, narrow], axis=0),
            preferred_element_type=jnp.float32,
        )
        first_out[first, 0:SPLIT, :] += product[:SPLIT]
        second_out[second, :, :] += product[SPLIT:]
        first_out[first, SPLIT:, :] += tile.reshape(16, 8, BLOCK).sum(0)

    tile_loop(count_ref, words, visit)


def backward_kernel(count_ref, target_ref, source_ref, bits_ref, *refs):
    *inputs, out_ref, pieces, stage, words, sems = refs

    def clear():
        out_ref[...] = jnp.zeros_like(out_ref)

    def prepare(block, carry):
        high, low = split_halves(stage[block])
        pieces[block, 0:BLOCK, :] = high
        pieces[block, BLOCK : 2 * BLOCK, :] = low
        return carry

    bring(inputs, stage, bits_ref, words, sems, clear, prepare)

    def visit(slot, tile):
        narrow = tile.astype(jnp.bfloat16)
        out_ref[target_ref[slot]] += jnp.dot(
            jnp.concatenate([narrow, narrow], axis=1),
            pieces[source_ref[slot]],
            preferred_element_type=jnp.float32,
        )

    tile_loop(count_ref, words, visit)


def run_tiles(kernel, scalars, bits, inputs, out_rows, name):
    blocks = sum(piece.shape[0] for piece in inputs)
    work = 2 * 2 * bits.shape[0] * BLOCK * BLOCK * 256
    return pl.pallas_call(
        kernel,
        out_shape=tuple(
            jax.ShapeDtypeStruct((blocks,) + shape, jnp.float32) for shape in out_rows
        ),
        in_specs=[SMEM] * len(scalars) + [ANY] * (1 + len(inputs)),
        out_specs=(VMEM,) * len(out_rows),
        scratch_shapes=[
            pltpu.VMEM((blocks, 256, 256), jnp.bfloat16),
            pltpu.VMEM((blocks,) + inputs[0].shape[1:], jnp.float32),
            pltpu.VMEM(bits.shape, jnp.int32),
            pltpu.SemaphoreType.DMA((len(inputs) + 1,)),
        ],
        compiler_params=pltpu.CompilerParams(vmem_limit_bytes=40 * 2**20),
        cost_estimate=pl.CostEstimate(
            flops=4 * work, bytes_accessed=10 * 2**20, transcendentals=0
        ),
        name=name,
    )(*scalars, bits, *inputs)


def digit_of(digit):
    axis, size, stride = digit
    return lax.axis_index(axis) // stride % size


def send(piece, digit, distance):
    axis, size, stride = digit
    pairs = []
    for index in range(lax.axis_size(axis)):
        own = index // stride % size
        pairs.append((index, index + ((own + distance) % size - own) * stride))
    return lax.ppermute(piece, axis, pairs)


def swap_gather(value, digit):
    return [value, send(value, digit, 1)]


def ring_gather(value, digit):
    half = value.shape[0] // 2
    before = send(value, digit, 1)
    after = send(value, digit, 3)
    far_first = send(before[:half], digit, 1)
    far_second = send(after[half:], digit, 3)
    return [value, after, far_first, far_second, before]


def quarters(value):
    rows = value.shape[0] // 4
    return (value[rows * k : rows * (k + 1)] for k in range(4))


def scatter_far(value, digit):
    _, _, far, _ = quarters(value)
    half = far.shape[0] // 2
    return send(far[:half], digit, 1), send(far[half:], digit, 3)


def scatter_near(value, digit, arrived):
    near, up, _, down = quarters(value)
    first, second = arrived
    half = near.shape[0] // 2
    up = send(jnp.concatenate([up[:half] + first, up[half:]]), digit, 1)
    down = send(jnp.concatenate([down[:half], down[half:] + second]), digit, 3)
    return near + up + down


def swap_scatter(value, digit):
    half = value.shape[0] // 2
    return value[:half] + send(value[half:], digit, 1)


def gather_row(value):
    near = jnp.concatenate(ring_gather(value, RING_Y))
    far = jnp.concatenate(ring_gather(send(value, PAIR, 1), RING_Y))
    return swap_gather(near, CORE) + swap_gather(far, CORE)


def gather_row_place(block):
    shard = block // 2
    place = relative(PAIR, shard) * 2 + relative(CORE, shard)
    return (place * 4 + relative(RING_Y, shard)) * 2 + block % 2


def scatter_row_place(block):
    shard = block // 2
    place = relative(CORE, shard) * 4 + relative(RING_Y, shard)
    return (place * 2 + relative(PAIR, shard)) * 2 + block % 2


def gather_col(value):
    own, after, far_first, far_second, before = ring_gather(value, RING_Z)
    far = jnp.concatenate([far_first, far_second])
    pieces = []
    for piece in (own, jnp.concatenate([after, before]), far):
        pieces += ring_gather(piece, RING_X)
    return pieces


def gather_col_place(block):
    shard = block // 2
    along, across = relative(RING_Z, shard), relative(RING_X, shard)
    single = jnp.where(along == 0, 0, 12) + across
    double = 4 + across * 2 + along // 2
    return jnp.where(along % 2 == 1, double, single) * 2 + block % 2


def scatter_col(first, second):
    for one, two in ((RING_X, RING_Z), (RING_Z, RING_X)):
        far = lax.optimization_barrier(
            (scatter_far(first, one), scatter_far(second, two))
        )
        first, second = lax.optimization_barrier(
            (scatter_near(first, one, far[0]), scatter_near(second, two, far[1]))
        )
    return first, second


def scatter_col_place(block, digits):
    shard = block // 2
    place = relative(digits[0], shard) * 4 + relative(digits[1], shard)
    return place * 2 + block % 2


def relative(digit, number):
    _, size, stride = digit
    return (number // stride % size - digit_of(digit)) % size


def sum_parts(value, groups):
    for group in groups:
        size, digit = group[1], digit_of(group)
        rows = value.shape[0] // size

        def part(distance, value=value, rows=rows, digit=digit, size=size):
            start = (digit + distance) % size * rows
            return lax.dynamic_slice_in_dim(value, start, rows, 0)

        parts = [part(0)] + [
            send(part(distance), group, distance) for distance in range(1, size)
        ]
        value = sum(parts[1:], parts[0])
    return value


def sum_ring(value, digit):
    one, two, three = (send(value, digit, distance) for distance in (1, 2, 3))
    return (value + two) + (one + three)


def gather_ring(value, digit):
    size, own = digit[1], digit_of(digit)
    pieces = [value] + [send(value, digit, size - d) for d in range(1, size)]
    pieces = jnp.concatenate(pieces + pieces)
    rows = value.shape[0]
    return lax.dynamic_slice_in_dim(pieces, (size - own) % size * rows, rows * size, 0)


def scatter_row(value, weights):
    value = swap_scatter(value, CORE)
    value, weights = lax.optimization_barrier((value, weights))
    far, weights = lax.optimization_barrier(
        (scatter_far(value, RING_Y), sum_ring(weights, RING_Z))
    )
    value, weights = lax.optimization_barrier(
        (scatter_near(value, RING_Y, far), sum_ring(weights, RING_X))
    )
    value, weights = swap_scatter(value, PAIR), gather_ring(weights, RING_Y)
    return value, gather_ring(gather_ring(weights, PAIR), CORE)


def local(features, w_self, w_neigh, upstream, tile_coords, tile_count, tile_bits):
    devices = lax.axis_size("row")
    rows_dev, feat = features.shape
    per_dev = rows_dev // BLOCK
    bits = tile_bits[0, 0]
    row_block, col_block = tile_coords[0, 0, :, 0], tile_coords[0, 0, :, 1]
    swap = [
        (r * devices + c, c * devices + r) for r in range(devices) for c in range(devices)
    ]

    turned = features.reshape(per_dev, BLOCK, feat).swapaxes(1, 2)
    gathered = gather_row(turned)
    first, second = run_tiles(
        forward_kernel,
        (
            tile_count,
            scatter_col_place(row_block, (RING_X, RING_Z)),
            scatter_col_place(row_block, (RING_Z, RING_X)),
            gather_row_place(col_block),
        ),
        bits,
        gathered,
        ((SPLIT + DEGREE_ROWS, BLOCK), (feat - SPLIT, BLOCK)),
        "forward",
    )
    own = lax.ppermute(features, ("row", "col"), swap)
    first, second, own = lax.optimization_barrier((first, second, own))
    first, second = scatter_col(first, second)

    degree = first[:, SPLIT:, :].sum(1)
    inverse = 1.0 / jnp.maximum(degree, 1.0)
    total = jnp.concatenate([first[:, :SPLIT], second], axis=1)
    aggregate = (total * inverse[:, None, :]).swapaxes(1, 2).reshape(rows_dev, feat)
    inverse = inverse.reshape(rows_dev, 1)
    preact = jnp.dot(own, w_self, precision=HIGH) + jnp.dot(
        aggregate, w_neigh, precision=HIGH
    )
    gate = jax.nn.sigmoid(preact)
    hidden = preact * gate
    grad_pre = upstream * gate * (1.0 + preact * (1.0 - gate))

    scaled = grad_pre * inverse
    weights = jnp.dot(
        jnp.concatenate([own, aggregate], axis=1).T, grad_pre, precision=HIGH
    )
    scaled, weights = lax.optimization_barrier((scaled, weights))
    weights = sum_parts(weights, (CORE, PAIR, RING_Y))
    gathered = gather_col(scaled.reshape(per_dev, BLOCK, feat))
    gathered, weights = lax.optimization_barrier((gathered, weights))
    grad_own = lax.ppermute(grad_pre, ("row", "col"), swap)
    (back,) = run_tiles(
        backward_kernel,
        (tile_count, scatter_row_place(col_block), gather_col_place(row_block)),
        bits,
        gathered,
        ((BLOCK, feat),),
        "backward",
    )
    back, grad_own = lax.optimization_barrier((back, grad_own))
    back, weights = scatter_row(back, weights)
    back = back.reshape(rows_dev, feat)
    grad_features = jnp.dot(grad_own, w_self.T, precision=HIGH) + jnp.dot(
        back, w_neigh.T, precision=HIGH
    )
    return hidden, grad_features, weights[:feat], weights[feat:]


def solution(mesh):
    return jax.shard_map(
        local,
        mesh=mesh,
        in_specs=(
            P(("col", "row"), None),
            P(),
            P(),
            P(("row", "col"), None),
            P("row", "col", None, None),
            P("row", "col"),
            P("row", "col", None, None, None),
        ),
        out_specs=(P(("row", "col"), None), P(("col", "row"), None), P(), P()),
        check_vma=False,
    )
```
